32 devices in a mesh: slab: 8 (over z, y), chan: 4 (over x, core).
Axes of the slice: x: 2, y: 2, z: 4, core: 2. Of those that a mesh axis runs over, the one named last changes fastest.
Arguments:
- features: bfloat16 [4, 32, 128, 512], P(None, 'slab', 'chan'), may hold values from -6 to 6
- neighbours: int32 [32, 27], P('slab'), may hold values from -1 to 7, as said below
- face_lists: int32 [8, 2, 2], P('slab'), may hold values from -1 to 3, as said below
- weight_first: bfloat16 [27, 128, 128], P(None, None, 'chan'), may hold values from -0.109375 to 0.109375
- bias_first: float32 [128], P('chan'), may hold values from -3 to 3
- weight_second: bfloat16 [27, 128, 128], P(None, None, 'chan'), may hold values from -0.109375 to 0.109375
- bias_second: float32 [128], P('chan'), may hold values from -3 to 3
- level_embed: float32 [4, 128], P(None, 'chan'), may hold values from -3 to 3
Outputs:
- denoised: bfloat16 [4, 32, 128, 512], P(None, 'slab', 'chan')
The draws below stay inside these ranges and needn't reach their ends.
Inputs may be any that keep to these rules, and one draw needn't show every extreme that they name: `neighbours`: slab s holds in its used slots, in some order, the active bricks of its two brick layers at positions of a 8 x 8 grid; each layer has at most 2 active bricks. Rows of unused slots are all -1; a used slot names itself at offset 13. Offsets with dz = -1 from the bottom layer name the slab below (never for slab 0), dz = +1 from the top layer the slab above (never for the last slab). `face_lists`: entry [s, 0, c] is the slot of the active bottom-layer brick at position c, entry [s, 1, c] that of the top-layer brick; -1 where the position has no active brick. The slots of a slab's used bricks each appear once.
All inputs are finite; a program needn't handle non-finite values.
Results may differ from the reference program's by a relative error of at most 0.02.
Values may be sent and summed in bfloat16 or wider, within the bound.
A program may use at most 128 MiB of HBM per device.

```python
import jax
import jax.numpy as jnp
from jax import lax

C = 128
LEVELS = 4
EDGE = 8
GRID = 8
NB_DEV = 4
FACE = 2
SLABS = 8
BRICKS = 32
N_CHAN = 4


def layout(key):
    base = jax.random.fold_in(key, 31)
    k_spot, k_count, k_pick, k_rank = jax.random.split(base, 4)
    cells = GRID * GRID
    spots = jax.random.permutation(k_spot, cells)[:FACE].astype(jnp.int32)
    counts = jax.random.randint(k_count, (SLABS, 2), 1, FACE + 1).astype(jnp.int32)
    fullest = jax.random.randint(k_pick, (), 0, SLABS - 1)
    slab = jnp.arange(SLABS, dtype=jnp.int32)
    counts = jnp.where(((slab == fullest) | (slab == fullest + 1))[:, None], FACE, counts)
    counts = jnp.where((slab == (fullest + 2) % SLABS)[:, None], 1, counts)
    column = jnp.arange(FACE, dtype=jnp.int32)
    valid = column[None, None, :] < counts[:, :, None]
    entry = jnp.arange(NB_DEV, dtype=jnp.int32)
    ranks = jax.vmap(lambda k: jax.random.permutation(k, NB_DEV))(jax.random.split(k_rank, SLABS)).astype(jnp.int32)
    sort_key = jnp.where(valid.reshape(SLABS, NB_DEV), ranks, NB_DEV + entry[None, :])
    order = jnp.argsort(sort_key, axis=1, stable=True).astype(jnp.int32)
    slot_of = jnp.argsort(order, axis=1, stable=True).astype(jnp.int32)
    cell_ids = jnp.arange(cells, dtype=jnp.int32)
    match = spots[:, None] == cell_ids[None, :]
    holder = jnp.where(valid, slot_of.reshape(SLABS, 2, FACE) + 1, 0)
    slot_at = jnp.sum(holder[:, :, :, None] * match[None, None].astype(jnp.int32), axis=2) - 1
    col_of = jnp.sum(jnp.where(match, column[:, None] + 1, 0), axis=0) - 1
    prev_top = jnp.where(slab > 0, jnp.roll(counts[:, 1], 1), 0)
    next_bottom = jnp.where(slab < SLABS - 1, jnp.roll(counts[:, 0], -1), 0)
    row_pos = spots // GRID
    col_pos = spots % GRID
    tiers = jnp.arange(2, dtype=jnp.int32)
    results = []
    for dz in (-1, 0, 1):
        for dy in (-1, 0, 1):
            for dx in (-1, 0, 1):
                near_y = row_pos + dy
                near_x = col_pos + dx
                inside = (near_y >= 0) & (near_y < GRID) & (near_x >= 0) & (near_x < GRID)
                cell = jnp.clip(near_y, 0, GRID - 1) * GRID + jnp.clip(near_x, 0, GRID - 1)
                other = col_of[cell][None, None, :]
                level_z = tiers[:, None] + dz
                same = slot_at[:, jnp.clip(level_z, 0, 1), cell[None, :]]
                lower = jnp.where((other >= 0) & (other < prev_top[:, None, None]), NB_DEV + other, -1)
                upper = jnp.where((other >= 0) & (other < next_bottom[:, None, None]), NB_DEV + FACE + other, -1)
                value = jnp.where(level_z[None] < 0, lower, jnp.where(level_z[None] > 1, upper, same))
                value = jnp.where(inside[None, None, :], value, -1)
                results.append(value)
    table = jnp.stack(results, axis=-1)
    table = jnp.where(valid[..., None], table, -1).reshape(SLABS, NB_DEV, 27)
    table = jnp.take_along_axis(table, order[:, :, None], axis=1)
    lists = jnp.where(valid, slot_of.reshape(SLABS, 2, FACE), -1)
    return (table.reshape(SLABS * NB_DEV, 27).astype(jnp.int32), lists.astype(jnp.int32))


def draw_neighbours(key, part):
    return layout(key)[0]


def draw_face_lists(key, part):
    return layout(key)[1]


def block_scale(own_key, shape, cuts, least, top_value):
    factor_of, own = 1.0, jax.random.fold_in(own_key, 6)
    for position, shards_of in cuts:
        draws = jnp.exp(jax.random.uniform(jax.random.fold_in(own, position), (shards_of,), jnp.float32, least / len(cuts), top_value / len(cuts)))
        factor_of = factor_of * jnp.repeat(draws, shape[position] // shards_of).reshape([-1 if axis == position else 1 for axis in range(len(shape))])
    return factor_of


def noise(stream_key, dims, deviation, limit, shards=(), kind=jnp.bfloat16):
    values = jax.random.normal(stream_key, dims, jnp.float32) * deviation
    if len(shards) > 0:
        values = block_scale(stream_key, dims, shards, -0.22, 0.18) * values
    return jnp.clip(values, min=-limit, max=limit).astype(kind)


def setup_inputs(seed: int = 0) -> dict:
    arg_keys = jax.random.split(jax.random.key(seed), 9)
    features = noise(arg_keys[0], (LEVELS, BRICKS, C, EDGE * EDGE * EDGE), 1.0, 6.0, ((1, 8), (2, 4)))
    neighbours = draw_neighbours(jax.random.fold_in(arg_keys[8], 71), 0)
    face_lists = draw_face_lists(jax.random.fold_in(arg_keys[8], 71), 0)
    weight_first = noise(arg_keys[3], (27, C, C), (27 * C) ** -0.5, 0.109375, ((2, 4),))
    bias_first = noise(arg_keys[4], (C,), 0.5, 3.0, ((0, 4),), jnp.float32)
    weight_second = noise(arg_keys[5], (27, C, C), (27 * C) ** -0.5, 0.109375, ((2, 4),))
    bias_second = noise(arg_keys[6], (C,), 0.5, 3.0, ((0, 4),), jnp.float32)
    level_embed = noise(arg_keys[7], (LEVELS, C), 0.5, 3.0, ((1, 4),), jnp.float32)
    return dict(features=features, neighbours=neighbours, face_lists=face_lists, weight_first=weight_first, bias_first=bias_first, weight_second=weight_second, bias_second=bias_second, level_embed=level_embed)


def span(step):
    if step < 0:
        return 7, 8
    if step == 0:
        return 0, 8
    return 0, 1


def assemble(full_pool, low_pool, high_pool, full_index, low_index, high_index):
    layers = []
    for dz in (-1, 0, 1):
        rows = []
        for dy in (-1, 0, 1):
            pieces = []
            for dx in (-1, 0, 1):
                k = 9 * (dz + 1) + 3 * (dy + 1) + (dx + 1)
                y_lo, y_hi = span(dy)
                x_lo, x_hi = span(dx)
                if dz == 0:
                    source = full_pool[:, :, :, :, y_lo:y_hi, x_lo:x_hi]
                    index = full_index[:, k]
                elif dz < 0:
                    source = low_pool[:, :, :, None, y_lo:y_hi, x_lo:x_hi]
                    index = low_index[:, k]
                else:
                    source = high_pool[:, :, :, None, y_lo:y_hi, x_lo:x_hi]
                    index = high_index[:, k]
                pieces.append(jnp.take(source, index, axis=1))
            rows.append(jnp.concatenate(pieces, axis=5))
        layers.append(jnp.concatenate(rows, axis=4))
    return jnp.concatenate(layers, axis=3)


def global_table(neighbours, face_lists):
    table = neighbours.reshape(SLABS, NB_DEV, 27)
    slab = jnp.arange(SLABS, dtype=jnp.int32)[:, None, None]
    below = jnp.clip(slab - 1, 0, SLABS - 1)
    above = jnp.clip(slab + 1, 0, SLABS - 1)
    col_low = jnp.clip(table - NB_DEV, 0, FACE - 1)
    col_high = jnp.clip(table - NB_DEV - FACE, 0, FACE - 1)
    from_low = below * NB_DEV + face_lists[below, 1, col_low]
    from_high = above * NB_DEV + face_lists[above, 0, col_high]
    local = slab * NB_DEV + table
    glob = jnp.where(table < 0, BRICKS, jnp.where(table < NB_DEV, local, jnp.where(table < NB_DEV + FACE, from_low, from_high)))
    return glob.astype(jnp.int32)


def convolve(padded, weight):
    levels, count, group = padded.shape[0], padded.shape[1], padded.shape[2]
    acc = jnp.zeros((levels, count, weight.shape[1], 512), jnp.float32)
    for dz in (-1, 0, 1):
        for dy in (-1, 0, 1):
            for dx in (-1, 0, 1):
                k = 9 * (dz + 1) + 3 * (dy + 1) + (dx + 1)
                window = padded[:, :, :, 1 + dz:9 + dz, 1 + dy:9 + dy, 1 + dx:9 + dx].reshape(levels, count, group, 512)
                acc = acc + jnp.einsum('oc,lbcv->lbov', weight[k].astype(jnp.float32), window.astype(jnp.float32))
    return acc


def conv_layer(features, glob, mask, weight, bias, shift):
    pool = features.reshape(LEVELS, BRICKS, C, 8, 8, 8)
    pool = jnp.concatenate([pool, jnp.zeros((LEVELS, 1, C, 8, 8, 8), features.dtype)], axis=1)
    low = pool[:, :, :, 7]
    high = pool[:, :, :, 0]
    group = C // N_CHAN

    def one_slab(index):
        padded = assemble(pool, low, high, index, index, index)
        total = jnp.zeros((LEVELS, NB_DEV, C, 512), jnp.float32)
        for g in range(N_CHAN):
            part = convolve(padded[:, :, g * group:(g + 1) * group], weight[:, :, g * group:(g + 1) * group])
            rounded = lax.optimization_barrier(part.astype(jnp.bfloat16))
            total = total + rounded.astype(jnp.float32)
        return total

    totals = lax.map(one_slab, glob)
    totals = totals.transpose(1, 0, 2, 3, 4).reshape(LEVELS, BRICKS, C, 512)
    act = jax.nn.silu(totals + bias[None, None, :, None] + shift[:, None, :, None]) * mask[None, :, None, None]
    return act.astype(jnp.bfloat16)


def reference(features, neighbours, face_lists, weight_first, bias_first, weight_second, bias_second, level_embed):
    glob = global_table(neighbours, face_lists)
    mask = (neighbours[:, 13] >= 0).astype(jnp.float32)
    hidden = conv_layer(features, glob, mask, weight_first, bias_first, level_embed)
    no_shift = jnp.zeros((LEVELS, C), jnp.float32)
    return conv_layer(hidden, glob, mask, weight_second, bias_second, no_shift)
```

```python
import functools

import jax
import jax.numpy as jnp
from jax import lax
from jax.experimental import pallas as pl
from jax.experimental.pallas import tpu as pltpu
from jax.sharding import PartitionSpec as P

MESH = pl.DeviceIdType.MESH
EDGE = 8
PLANE = EDGE * EDGE
PARTS = 3


def kernel(
    slabs,
    feat, table, faces, small, wa, wb,
    out,
    xt, w_all, small_all, pool, even, odd, face_out, face_in, staged,
    feat_send, feat_recv, w_send, w_recv, small_send, small_recv,
    face_send, face_recv, out_send, out_recv, local_sem,
):
    levels, bricks, group, voxels = feat.shape
    face = faces.shape[1]
    channels = xt.shape[1]
    blank = bricks * EDGE + 2 * face
    s, g = lax.axis_index("slab"), lax.axis_index("chan")
    chip, core = g // 2, g % 2
    across = 2 * (1 - chip) + core
    diagonal = 2 * (1 - chip) + (1 - core)
    twin = 2 * chip + (1 - core)
    peers = (across, diagonal, twin)
    has_below, has_above = s > 0, s < slabs - 1

    barrier = pltpu.get_barrier_semaphore()
    for peer in peers:
        pl.semaphore_signal(barrier, inc=1, device_id=(s, peer), device_id_type=MESH)

    @pl.when(has_below)
    def _():
        pl.semaphore_signal(barrier, inc=1, device_id=(s - 1, g), device_id_type=MESH)

    @pl.when(has_above)
    def _():
        pl.semaphore_signal(barrier, inc=1, device_id=(s + 1, g), device_id_type=MESH)

    sides = (s + slabs - 1) // slabs + (2 * slabs - 2 - s) // slabs
    pl.semaphore_wait(barrier, len(peers) + sides)

    def rows(owner):
        return pl.ds(pl.multiple_of(owner * group, group), group)

    def remote(src, dst, send, recv, peer):
        return pltpu.make_async_remote_copy(
            src_ref=src, dst_ref=dst, send_sem=send, recv_sem=recv,
            device_id=peer, device_id_type=MESH,
        )

    def feat_copy(j):
        return remote(
            feat.at[peers[j]], xt.at[:, rows(g), :], feat_send.at[j], feat_recv.at[j],
            (s, peers[j]),
        )

    per = 27 // PARTS

    def w_own(layer, part, j):
        taps = pl.ds(part * per, per)
        source = (wa, wb)[layer]
        return remote(
            source.at[taps], w_all.at[layer, taps, rows(g), :],
            w_send.at[layer, part, j], w_recv.at[layer, part, j],
            (s, (across, twin)[j]),
        )

    def w_forward(layer, part):
        taps = pl.ds(part * per, per)
        block = w_all.at[layer, taps, rows(across), :]
        return remote(
            block, block, w_send.at[layer, part, 2], w_recv.at[layer, part, 2], (s, twin)
        )

    def small_copy(j):
        return remote(
            small, small_all.at[g], small_send.at[j], small_recv.at[j], (s, peers[j])
        )

    for j in range(3):
        feat_copy(j).start()
    for j in range(3):
        small_copy(j).start()
    for part in range(PARTS):
        for j in range(2):
            w_own(0, part, j).start()
    for part in range(PARTS):
        for j in range(2):
            w_own(1, part, j).start()
    own_feat = pltpu.make_async_copy(feat.at[g], xt.at[:, rows(g), :], local_sem.at[0])
    own_wa = pltpu.make_async_copy(wa, w_all.at[0, :, rows(g), :], local_sem.at[1])
    own_wb = pltpu.make_async_copy(wb, w_all.at[1, :, rows(g), :], local_sem.at[2])
    own_feat.start()
    own_wa.start()
    own_wb.start()
    small_all[g] = small[...]
    pool[:, pl.ds(bricks * EDGE, 2 * face + 1)] = jnp.zeros(
        (2, 2 * face + 1, EDGE, EDGE, channels), jnp.float32
    )
    own_feat.wait()
    for j in range(3):
        feat_copy(j).wait()

    def fill(b, carry):
        turned = xt[b].astype(jnp.float32).T
        pool[0, pl.ds(b * EDGE, EDGE)] = turned.reshape(EDGE, EDGE, EDGE, channels)
        return carry

    lax.fori_loop(0, bricks, fill, 0)

    def face_copy(layer, way):
        target = (s + 1, g) if way == 0 else (s - 1, g)
        return remote(
            face_out.at[layer, way], face_in.at[layer, way],
            face_send.at[layer, way], face_recv.at[layer, way], target,
        )

    def send_faces(layer):
        for way, entry, z in ((0, 1, EDGE - 1), (1, 0, 0)):
            for c in range(face):
                slot = jnp.maximum(faces[entry, c], 0)
                chosen = pool[layer, slot * EDGE + z]
                face_out[layer, way, c] = chosen.reshape(PLANE, channels).astype(jnp.bfloat16)

        @pl.when(has_above)
        def _():
            face_copy(layer, 0).start()

        @pl.when(has_below)
        def _():
            face_copy(layer, 1).start()

    def land(layer, way):
        first = bricks * EDGE + way * face
        landed = face_in[layer, way].astype(jnp.float32)
        pool[layer, pl.ds(first, face)] = landed.reshape(face, EDGE, EDGE, channels)

    def receive_faces(layer):
        @pl.when(has_above)
        def _():
            face_copy(layer, 0).wait_send()
            face_copy(layer, 1).wait_recv()
            land(layer, 1)

        @pl.when(has_below)
        def _():
            face_copy(layer, 1).wait_send()
            face_copy(layer, 0).wait_recv()
            land(layer, 0)

    spot = lax.broadcasted_iota(jnp.int32, (EDGE + 2, EDGE, channels), 1)

    def build_plane(layer, b, zp):
        dz = jnp.where(zp == 0, -1, jnp.where(zp == EDGE + 1, 1, 0))
        z = (zp + EDGE - 1) % EDGE

        def strip(dx):
            pieces = []
            for dy in (-1, 0, 1):
                t = table[b, 9 * (dz + 1) + 3 * (dy + 1) + (dx + 1)]
                where = jnp.where(
                    t < 0, blank, jnp.where(t < bricks, t * EDGE + z, bricks * (EDGE - 1) + t)
                )
                got = pool[layer, where]
                pieces.append(got[EDGE - 1 :] if dy < 0 else got if dy == 0 else got[:1])
            return jnp.concatenate(pieces, axis=0)

        left, middle, right = strip(-1), strip(0), strip(1)
        before = pltpu.roll(jnp.where(spot == EDGE - 1, left, middle), 1, 1)
        after = pltpu.roll(jnp.where(spot == 0, right, middle), EDGE - 1, 1)
        for j, value in enumerate((before, middle, after)):
            even[j, b, zp] = value.reshape((EDGE + 2) * EDGE, channels).astype(jnp.bfloat16)
            odd[j, b, zp] = value[1:-1].reshape(PLANE, channels).astype(jnp.bfloat16)

    def build_inner(layer):
        def step(i, carry):
            build_plane(layer, i // EDGE, i % EDGE + 1)
            return carry

        lax.fori_loop(0, bricks * EDGE, step, 0)

    def build_outer(layer):
        def step(b, carry):
            build_plane(layer, b, 0)
            build_plane(layer, b, EDGE + 1)
            return carry

        lax.fori_loop(0, bricks, step, 0)

    def convolve(layer, b):
        acc = None
        for dz in range(3):
            pieces = []
            for dy in range(3):
                for dx in range(3):
                    if dy == 1:
                        piece = odd[dx, b, pl.ds(dz, EDGE)]
                    else:
                        piece = even[dx, b, pl.ds(dz, EDGE), pl.ds(dy * EDGE, PLANE)]
                    pieces.append(piece.reshape(voxels, channels))
            taps = w_all[layer, pl.ds(9 * dz, 9)].reshape(9 * channels, channels)
            part = jnp.dot(
                jnp.concatenate(pieces, axis=1), taps, preferred_element_type=jnp.float32
            )
            acc = part if acc is None else acc + part
        return acc

    def activate(total, b):
        on = jnp.where(table[b, 13] >= 0, 1.0, 0.0)
        return total * (0.5 * on) * (1.0 + jnp.tanh(0.5 * total))

    def gather_weights(layer):
        for part in range(PARTS):
            w_own(layer, part, 0).wait_recv()
            w_forward(layer, part).start()
        for part in range(PARTS):
            w_own(layer, part, 1).wait_recv()
            w_forward(layer, part).wait()
            w_own(layer, part, 0).wait_send()
            w_own(layer, part, 1).wait_send()

    send_faces(0)
    build_inner(0)
    receive_faces(0)
    build_outer(0)
    for j in range(3):
        small_copy(j).wait()
    own_wa.wait()
    gather_weights(0)
    shared = jnp.sum(small_all[...], axis=0)
    row = lax.broadcasted_iota(jnp.int32, shared.shape, 0)
    shift = jnp.sum(jnp.where(row == g, shared, 0.0), axis=0, keepdims=True)
    last = shared[levels : levels + 1]

    def first(b, carry):
        act = activate(convolve(0, b) + shift, b).astype(jnp.bfloat16).astype(jnp.float32)
        pool[1, pl.ds(b * EDGE, EDGE)] = act.reshape(EDGE, EDGE, EDGE, channels)
        return carry

    lax.fori_loop(0, bricks, first, 0)
    send_faces(1)
    build_inner(1)
    receive_faces(1)
    build_outer(1)
    own_wb.wait()
    gather_weights(1)

    def out_copy(b, j):
        return remote(
            staged.at[b, rows(peers[j])], out.at[g, b], out_send.at[b, j], out_recv.at[b, j],
            (s, peers[j]),
        )

    def second(b, carry):
        act = activate(convolve(1, b) + last, b)
        staged[b] = act.T.astype(jnp.bfloat16)
        for j in range(3):
            out_copy(b, j).start()
        out[g, b] = staged[b, rows(g)]
        return carry

    lax.fori_loop(0, bricks, second, 0)

    def finish(b, carry):
        for j in range(3):
            out_copy(b, j).wait()
        return carry

    lax.fori_loop(0, bricks, finish, 0)


def shards(features, neighbours, face_lists, weight_first, bias_first, weight_second, bias_second, level_embed):
    levels, bricks, group, voxels = features.shape
    n_chan = lax.axis_size("chan")
    channels = group * n_chan
    face = face_lists.shape[2]
    rows = jnp.concatenate(
        [bias_first[None] + level_embed, bias_second[None], jnp.zeros((3, group), jnp.float32)]
    )
    lane = lax.broadcasted_iota(jnp.int32, (8, channels), 1)
    small = jnp.where(lane // group == lax.axis_index("chan"), jnp.tile(rows, (1, n_chan)), 0.0)
    planes = bricks * EDGE + 2 * face + 1
    dma = pltpu.SemaphoreType.DMA
    vmem = pl.BlockSpec(memory_space=pltpu.VMEM)
    smem = pl.BlockSpec(memory_space=pltpu.SMEM)
    return pl.pallas_call(
        functools.partial(kernel, lax.axis_size("slab")),
        out_shape=jax.ShapeDtypeStruct(features.shape, features.dtype),
        in_specs=[vmem, smem, smem, vmem, vmem, vmem],
        out_specs=vmem,
        scratch_shapes=[
            pltpu.VMEM((bricks, channels, voxels), jnp.bfloat16),
            pltpu.VMEM((2, 27, channels, channels), jnp.bfloat16),
            pltpu.VMEM((n_chan, 8, channels), jnp.float32),
            pltpu.VMEM((2, planes, EDGE, EDGE, channels), jnp.float32),
            pltpu.VMEM((3, bricks, EDGE + 2, (EDGE + 2) * EDGE, channels), jnp.bfloat16),
            pltpu.VMEM((3, bricks, EDGE + 2, PLANE, channels), jnp.bfloat16),
            pltpu.VMEM((2, 2, face, PLANE, channels), jnp.bfloat16),
            pltpu.VMEM((2, 2, face, PLANE, channels), jnp.bfloat16),
            pltpu.VMEM((bricks, channels, voxels), jnp.bfloat16),
            dma((3,)), dma((3,)),
            dma((2, PARTS, 3)), dma((2, PARTS, 3)),
            dma((3,)), dma((3,)),
            dma((2, 2)), dma((2, 2)),
            dma((bricks, 3)), dma((bricks, 3)),
            dma((3,)),
        ],
        compiler_params=pltpu.CompilerParams(
            collective_id=0, has_side_effects=True, vmem_limit_bytes=48 * 1024 * 1024
        ),
        cost_estimate=pl.CostEstimate(
            flops=4 * 27 * channels * channels * bricks * voxels,
            bytes_accessed=4 * features.size,
            transcendentals=2 * channels * bricks * voxels,
        ),
    )(
        features, neighbours, face_lists[0], small,
        weight_first.transpose(0, 2, 1), weight_second.transpose(0, 2, 1),
    )


def solution(mesh):
    placed = (
        P(None, "slab", "chan", None),
        P("slab", None),
        P("slab", None, None),
        P(None, None, "chan"),
        P("chan"),
        P(None, None, "chan"),
        P("chan"),
        P(None, "chan"),
    )
    return jax.shard_map(
        shards, mesh=mesh, in_specs=placed, out_specs=P(None, "slab", "chan", None), check_vma=False
    )
```

```python
import functools

import jax
import jax.numpy as jnp
from jax import lax
from jax.experimental import pallas as pl
from jax.experimental.pallas import tpu as pltpu
from jax.sharding import PartitionSpec as P

MESH = pl.DeviceIdType.MESH
EDGE = 8
PLANE = EDGE * EDGE
PARTS = 3
VMEM_LIMIT = 64 * 1024 * 1024


def kernel(
    slabs,
    feat, table_in, faces_in, first_bias, second_bias, embed, wa, wb,
    out,
    table, faces, first_bias_here, second_bias_here, embed_here, small,
    xt, w_all, small_all, pool, even, odd, acc, face_out, face_in, staged,
    feat_send, feat_recv, w_send, w_recv, small_send, small_recv,
    face_send, face_recv, out_send, out_recv, local_sem, own_sem,
):
    levels, bricks, group, voxels = feat.shape
    face = faces.shape[2]
    channels = xt.shape[1]
    blank = bricks * EDGE
    edges = blank + EDGE
    s, g = lax.axis_index("slab"), lax.axis_index("chan")
    chip, core = g // 2, g % 2
    across = 2 * (1 - chip) + core
    diagonal = 2 * (1 - chip) + (1 - core)
    twin = 2 * chip + (1 - core)
    peers = (across, diagonal, twin)
    has_below, has_above = s > 0, s < slabs - 1

    def rows(owner):
        return pl.ds(pl.multiple_of(owner * group, group), group)

    def local(i, source, target):
        return pltpu.make_async_copy(source, target, local_sem.at[i])

    here = [
        local(0, feat.at[g], xt.at[:, rows(g), :]),
        local(1, first_bias, first_bias_here),
        local(2, second_bias, second_bias_here),
        local(3, embed, embed_here),
        local(4, table_in, table),
        local(5, faces_in, faces),
        local(6, wa, w_all.at[0, :, rows(g), :]),
        local(7, wb, w_all.at[1, :, rows(g), :]),
    ]
    for copy in here:
        copy.start()

    barrier = pltpu.get_barrier_semaphore()
    for peer in peers:
        pl.semaphore_signal(barrier, inc=1, device_id=(s, peer), device_id_type=MESH)

    @pl.when(has_below)
    def _():
        pl.semaphore_signal(barrier, inc=1, device_id=(s - 1, g), device_id_type=MESH)

    @pl.when(has_above)
    def _():
        pl.semaphore_signal(barrier, inc=1, device_id=(s + 1, g), device_id_type=MESH)

    sides = (s + slabs - 1) // slabs + (2 * slabs - 2 - s) // slabs
    pl.semaphore_wait(barrier, len(peers) + sides)

    def remote(src, dst, send, recv, peer):
        return pltpu.make_async_remote_copy(
            src_ref=src, dst_ref=dst, send_sem=send, recv_sem=recv,
            device_id=peer, device_id_type=MESH,
        )

    def feat_copy(b, j):
        return remote(
            feat.at[peers[j], b], xt.at[b, rows(g), :], feat_send.at[b, j], feat_recv.at[b, j],
            (s, peers[j]),
        )

    per = 27 // PARTS

    def w_own(layer, part, j):
        taps = pl.ds(part * per, per)
        source = (wa, wb)[layer]
        return remote(
            source.at[taps], w_all.at[layer, taps, rows(g), :],
            w_send.at[layer, part, j], w_recv.at[layer, part, j],
            (s, (across, twin)[j]),
        )

    def w_forward(layer, part):
        taps = pl.ds(part * per, per)
        block = w_all.at[layer, taps, rows(across), :]
        return remote(
            block, block, w_send.at[layer, part, 2], w_recv.at[layer, part, 2], (s, twin)
        )

    def small_copy(j):
        return remote(
            small, small_all.at[g], small_send.at[j], small_recv.at[j], (s, peers[j])
        )

    def send_weights(layer, parts):
        for part in parts:
            for j in range(2):
                w_own(layer, part, j).start()

    for b in range(bricks):
        for j in range(3):
            feat_copy(b, j).start()
    for i in (1, 2, 3):
        here[i].wait()
    width = first_bias_here.shape[1]
    mine = jnp.concatenate(
        [
            first_bias_here[...] + embed_here[...],
            second_bias_here[...],
            jnp.zeros((7 - levels, width), jnp.float32),
        ],
        axis=0,
    )
    lane = lax.broadcasted_iota(jnp.int32, (8, channels), 1)
    spread = jnp.concatenate([mine] * (channels // width), axis=1)
    small[...] = jnp.where(lane // group == g, spread, 0.0)
    for j in range(3):
        small_copy(j).start()
    small_all[g] = small[...]
    pool[:, pl.ds(blank, EDGE + 2 * face)] = jnp.zeros(
        (2, EDGE + 2 * face, EDGE, EDGE, channels), jnp.float32
    )
    here[0].wait()
    for b in range(bricks):
        for j in range(3):
            feat_copy(b, j).wait_recv()
        turned = xt[b].astype(jnp.float32).T
        pool[0, pl.ds(b * EDGE, EDGE)] = turned.reshape(EDGE, EDGE, EDGE, channels)
        if b == bricks // 2 - 1:
            send_weights(0, (1,))
    send_weights(0, (0, 2))
    for i in (4, 5):
        here[i].wait()

    def face_copy(layer, way):
        target = (s + 1, g) if way == 0 else (s - 1, g)
        return remote(
            face_out.at[layer, way], face_in.at[layer, way],
            face_send.at[layer, way], face_recv.at[layer, way], target,
        )

    def send_faces(layer):
        for way, entry, z in ((0, 1, EDGE - 1), (1, 0, 0)):
            for c in range(face):
                slot = jnp.maximum(faces[0, entry, c], 0)
                chosen = pool[layer, slot * EDGE + z]
                face_out[layer, way, c] = chosen.reshape(PLANE, channels).astype(jnp.bfloat16)

        @pl.when(has_above)
        def _():
            face_copy(layer, 0).start()

        @pl.when(has_below)
        def _():
            face_copy(layer, 1).start()

    def land(layer, way):
        first = edges + way * face
        landed = face_in[layer, way].astype(jnp.float32)
        pool[layer, pl.ds(first, face)] = landed.reshape(face, EDGE, EDGE, channels)

    def receive_faces(layer):
        @pl.when(has_above)
        def _():
            face_copy(layer, 0).wait_send()
            face_copy(layer, 1).wait_recv()
            land(layer, 1)

        @pl.when(has_below)
        def _():
            face_copy(layer, 1).wait_send()
            face_copy(layer, 0).wait_recv()
            land(layer, 0)

    spot = lax.broadcasted_iota(jnp.int32, (EDGE + 2, EDGE, channels), 1)

    def build_plane(layer, b, dz, z):
        def strip(dx):
            pieces = []
            for dy in (-1, 0, 1):
                t = table[b, 9 * (dz + 1) + 3 * (dy + 1) + (dx + 1)]
                place = jnp.where(t < 0, blank, t * EDGE) + z
                if dz != 0:
                    place = jnp.where(t < bricks, place, edges - bricks + t)
                got = pool[layer, place]
                pieces.append(got[EDGE - 1 :] if dy < 0 else got if dy == 0 else got[:1])
            return jnp.concatenate(pieces, axis=0)

        left, middle, right = strip(-1), strip(0), strip(1)
        before = pltpu.roll(jnp.where(spot == EDGE - 1, left, middle), 1, 1)
        after = pltpu.roll(jnp.where(spot == 0, right, middle), EDGE - 1, 1)
        zp = z + 1 + EDGE * dz
        for j, value in enumerate((before, middle, after)):
            even[j, b, zp] = value.reshape((EDGE + 2) * EDGE, channels).astype(jnp.bfloat16)
            odd[j, b, zp] = value[1:-1].reshape(PLANE, channels).astype(jnp.bfloat16)

    def build_inner(layer):
        def step(b, carry):
            for z in range(EDGE):
                build_plane(layer, b, 0, z)
            return carry

        lax.fori_loop(0, bricks, step, 0)

    def build_outer(layer):
        def step(b, carry):
            build_plane(layer, b, -1, EDGE - 1)
            build_plane(layer, b, 1, 0)
            return carry

        lax.fori_loop(0, bricks, step, 0)

    def operand(b, first, count):
        pieces = []
        for dy in range(3):
            for dx in range(3):
                if dy == 1:
                    piece = odd[dx, b, pl.ds(first, count)]
                else:
                    piece = even[dx, b, pl.ds(first, count), pl.ds(dy * EDGE, PLANE)]
                pieces.append(piece.reshape(count * PLANE, channels))
        return jnp.concatenate(pieces, axis=1)

    def taps_of(layer, dz):
        return w_all[layer, pl.ds(9 * dz, 9)].reshape(9 * channels, channels)

    def middle_products(layer):
        def step(b, carry):
            acc[b] = jnp.dot(
                operand(b, 1, EDGE), taps_of(layer, 1), preferred_element_type=jnp.float32
            )
            return carry

        lax.fori_loop(0, bricks, step, 0)

    def convolve(layer, b):
        both = jnp.concatenate([taps_of(layer, 0), taps_of(layer, 2)], axis=1)
        wide = jnp.dot(operand(b, 0, EDGE + 2), both, preferred_element_type=jnp.float32)
        return acc[b] + wide[:voxels, :channels] + wide[2 * PLANE :, channels:]

    def activate(total, b):
        on = jnp.where(table[b, 13] >= 0, 1.0, 0.0)
        return total * (0.5 * on) * (1.0 + jnp.tanh(0.5 * total))

    def gather_weights(layer, parts):
        for part in parts:
            w_own(layer, part, 0).wait_recv()
            w_forward(layer, part).start()
        for part in parts:
            w_own(layer, part, 1).wait_recv()
            w_forward(layer, part).wait()
            w_own(layer, part, 0).wait_send()
            w_own(layer, part, 1).wait_send()

    send_faces(0)
    build_inner(0)
    send_weights(1, (1, 0, 2))
    here[6].wait()
    gather_weights(0, (1,))
    middle_products(0)
    receive_faces(0)
    build_outer(0)
    gather_weights(0, (0, 2))
    for j in range(3):
        small_copy(j).wait()
    shared = jnp.sum(small_all[...], axis=0)
    row = lax.broadcasted_iota(jnp.int32, shared.shape, 0)
    shift = jnp.sum(jnp.where(row == g, shared, 0.0), axis=0, keepdims=True)
    last = shared[levels : levels + 1]

    def first(b, carry):
        act = activate(convolve(0, b) + shift, b).astype(jnp.bfloat16).astype(jnp.float32)
        pool[1, pl.ds(b * EDGE, EDGE)] = act.reshape(EDGE, EDGE, EDGE, channels)
        return carry

    lax.fori_loop(0, bricks, first, 0)
    send_faces(1)
    build_inner(1)
    here[7].wait()
    gather_weights(1, (1, 0, 2))
    middle_products(1)
    receive_faces(1)
    build_outer(1)

    def out_copy(b, j):
        return remote(
            staged.at[b, rows(peers[j])], out.at[g, b], out_send.at[b, j], out_recv.at[b, j],
            (s, peers[j]),
        )

    def out_here(b):
        return pltpu.make_async_copy(staged.at[b, rows(g)], out.at[g, b], own_sem.at[b])

    def second(b, carry):
        act = activate(convolve(1, b) + last, b)
        staged[b] = act.T.astype(jnp.bfloat16)
        for j in range(3):
            out_copy(b, j).start()
        out_here(b).start()
        return carry

    lax.fori_loop(0, bricks, second, 0)

    def finish(b, carry):
        out_here(b).wait()
        for j in range(3):
            out_copy(b, j).wait()
            feat_copy(b, j).wait_send()
        return carry

    lax.fori_loop(0, bricks, finish, 0)


def shards(features, neighbours, face_lists, weight_first, bias_first, weight_second, bias_second, level_embed):
    levels, bricks, group, voxels = features.shape
    n_chan = lax.axis_size("chan")
    channels = group * n_chan
    face = face_lists.shape[2]
    planes = bricks * EDGE + EDGE + 2 * face
    dma = pltpu.SemaphoreType.DMA
    return pl.pallas_call(
        functools.partial(kernel, lax.axis_size("slab")),
        out_shape=jax.ShapeDtypeStruct(features.shape, features.dtype),
        in_specs=[pl.BlockSpec(memory_space=pl.ANY)] * 8,
        out_specs=pl.BlockSpec(memory_space=pl.ANY),
        scratch_shapes=[
            pltpu.SMEM(neighbours.shape, jnp.int32),
            pltpu.SMEM(face_lists.shape, jnp.int32),
            pltpu.VMEM((1, group), jnp.float32),
            pltpu.VMEM((1, group), jnp.float32),
            pltpu.VMEM((levels, group), jnp.float32),
            pltpu.VMEM((8, channels), jnp.float32),
            pltpu.VMEM((bricks, channels, voxels), jnp.bfloat16),
            pltpu.VMEM((2, 27, channels, channels), jnp.bfloat16),
            pltpu.VMEM((n_chan, 8, channels), jnp.float32),
            pltpu.VMEM((2, planes, EDGE, EDGE, channels), jnp.float32),
            pltpu.VMEM((3, bricks, EDGE + 2, (EDGE + 2) * EDGE, channels), jnp.bfloat16),
            pltpu.VMEM((3, bricks, EDGE + 2, PLANE, channels), jnp.bfloat16),
            pltpu.VMEM((bricks, voxels, channels), jnp.float32),
            pltpu.VMEM((2, 2, face, PLANE, channels), jnp.bfloat16),
            pltpu.VMEM((2, 2, face, PLANE, channels), jnp.bfloat16),
            pltpu.VMEM((bricks, channels, voxels), jnp.bfloat16),
            dma((bricks, 3)), dma((bricks, 3)),
            dma((2, PARTS, 3)), dma((2, PARTS, 3)),
            dma((3,)), dma((3,)),
            dma((2, 2)), dma((2, 2)),
            dma((bricks, 3)), dma((bricks, 3)),
            dma((8,)), dma((bricks,)),
        ],
        compiler_params=pltpu.CompilerParams(
            collective_id=0, has_side_effects=True, vmem_limit_bytes=VMEM_LIMIT
        ),
        cost_estimate=pl.CostEstimate(
            flops=4 * 27 * channels * channels * bricks * voxels,
            bytes_accessed=4 * features.size,
            transcendentals=2 * channels * bricks * voxels,
        ),
    )(
        features, neighbours, face_lists, bias_first[None], bias_second[None], level_embed,
        weight_first.transpose(0, 2, 1), weight_second.transpose(0, 2, 1),
    )


def solution(mesh):
    placed = (
        P(None, "slab", "chan", None),
        P("slab", None),
        P("slab", None, None),
        P(None, None, "chan"),
        P("chan"),
        P(None, None, "chan"),
        P("chan"),
        P(None, "chan"),
    )
    return jax.shard_map(
        shards, mesh=mesh, in_specs=placed, out_specs=P(None, "slab", "chan", None), check_vma=False
    )
```

```python
import functools

import jax
import jax.numpy as jnp
from jax import lax
from jax.experimental import pallas as pl
from jax.experimental.pallas import tpu as pltpu
from jax.sharding import PartitionSpec as P

MESH = pl.DeviceIdType.MESH
EDGE = 8
PLANE = EDGE * EDGE
PARTS = 3
LANES = 128
ORDER = (0, 3, 1, 2)
VMEM_LIMIT = 63 * 1024 * 1024


def kernel(
    slabs,
    feat, table_in, faces_in, first_bias, second_bias, embed, wa, wb,
    out,
    table, faces, first_bias_here, second_bias_here, embed_here, small,
    xt, w_all, small_all, pool, even, odd, acc, face_out, face_in, staged,
    feat_send, feat_recv, w_send, w_recv, small_send, small_recv,
    face_send, face_recv, out_send, out_recv, local_sem, own_sem,
):
    levels, bricks, group, voxels = feat.shape
    face = faces.shape[2]
    channels = xt.shape[1]
    blank = bricks * EDGE
    edges = blank + EDGE
    s, g = lax.axis_index("slab"), lax.axis_index("chan")
    chip, core = g // 2, g % 2
    across = 2 * (1 - chip) + core
    diagonal = 2 * (1 - chip) + (1 - core)
    twin = 2 * chip + (1 - core)
    peers = (across, diagonal, twin)
    has_below, has_above = s > 0, s < slabs - 1

    def rows(owner):
        return pl.ds(pl.multiple_of(owner * group, group), group)

    def local(i, source, target):
        return pltpu.make_async_copy(source, target, local_sem.at[i])

    here = [
        local(0, feat.at[g], xt.at[:, rows(g), :]),
        local(1, first_bias, first_bias_here),
        local(2, second_bias, second_bias_here),
        local(3, embed, embed_here),
        local(4, table_in, table),
        local(5, faces_in, faces),
        local(6, wa, w_all.at[0, :, rows(g), :]),
        local(7, wb, w_all.at[1, :, rows(g), :]),
    ]
    for copy in here:
        copy.start()

    barrier = pltpu.get_barrier_semaphore()
    for peer in peers:
        pl.semaphore_signal(barrier, inc=1, device_id=(s, peer), device_id_type=MESH)

    @pl.when(has_below)
    def _():
        pl.semaphore_signal(barrier, inc=1, device_id=(s - 1, g), device_id_type=MESH)

    @pl.when(has_above)
    def _():
        pl.semaphore_signal(barrier, inc=1, device_id=(s + 1, g), device_id_type=MESH)

    sides = (s + slabs - 1) // slabs + (2 * slabs - 2 - s) // slabs
    pl.semaphore_wait(barrier, len(peers) + sides)

    def remote(src, dst, send, recv, peer):
        return pltpu.make_async_remote_copy(
            src_ref=src, dst_ref=dst, send_sem=send, recv_sem=recv,
            device_id=peer, device_id_type=MESH,
        )

    def feat_copy(q, j):
        part = pl.ds(q * LANES, LANES)
        return remote(
            feat.at[peers[j], :, :, part], xt.at[:, rows(g), part],
            feat_send.at[q, j], feat_recv.at[q, j], (s, peers[j]),
        )

    per = 27 // PARTS

    def w_own(layer, part, j):
        taps = pl.ds(part * per, per)
        source = (wa, wb)[layer]
        return remote(
            source.at[taps], w_all.at[layer, taps, rows(g), :],
            w_send.at[layer, part, j], w_recv.at[layer, part, j],
            (s, (across, twin)[j]),
        )

    def w_forward(layer, part):
        taps = pl.ds(part * per, per)
        block = w_all.at[layer, taps, rows(across), :]
        return remote(
            block, block, w_send.at[layer, part, 2], w_recv.at[layer, part, 2], (s, twin)
        )

    def small_copy(j):
        return remote(
            small, small_all.at[g], small_send.at[j], small_recv.at[j], (s, peers[j])
        )

    def send_weights(layer, parts):
        for part in parts:
            for j in range(2):
                w_own(layer, part, j).start()

    for q in ORDER:
        for j in range(3):
            feat_copy(q, j).start()
    for i in (1, 2, 3):
        here[i].wait()
    width = first_bias_here.shape[1]
    mine = jnp.concatenate(
        [
            first_bias_here[...] + embed_here[...],
            second_bias_here[...],
            jnp.zeros((7 - levels, width), jnp.float32),
        ],
        axis=0,
    )
    lane = lax.broadcasted_iota(jnp.int32, (8, channels), 1)
    spread = jnp.concatenate([mine] * (channels // width), axis=1)
    small[...] = jnp.where(lane // group == g, spread, 0.0)
    for j in range(3):
        small_copy(j).start()
    small_all[g] = small[...]
    pool[:, pl.ds(blank, EDGE + 2 * face)] = jnp.zeros(
        (2, EDGE + 2 * face, EDGE, EDGE, channels), jnp.float32
    )
    def face_copy(layer, way):
        target = (s + 1, g) if way == 0 else (s - 1, g)
        return remote(
            face_out.at[layer, way], face_in.at[layer, way],
            face_send.at[layer, way], face_recv.at[layer, way], target,
        )

    def send_faces(layer):
        for way, entry, z in ((0, 1, EDGE - 1), (1, 0, 0)):
            for c in range(face):
                slot = jnp.maximum(faces[0, entry, c], 0)
                chosen = pool[layer, slot * EDGE + z]
                face_out[layer, way, c] = chosen.reshape(PLANE, channels).astype(jnp.bfloat16)

        @pl.when(has_above)
        def _():
            face_copy(layer, 0).start()

        @pl.when(has_below)
        def _():
            face_copy(layer, 1).start()

    def land(layer, way):
        first = edges + way * face
        landed = face_in[layer, way].astype(jnp.float32)
        pool[layer, pl.ds(first, face)] = landed.reshape(face, EDGE, EDGE, channels)

    def receive_faces(layer):
        @pl.when(has_above)
        def _():
            face_copy(layer, 0).wait_send()
            face_copy(layer, 1).wait_recv()
            land(layer, 1)

        @pl.when(has_below)
        def _():
            face_copy(layer, 1).wait_send()
            face_copy(layer, 0).wait_recv()
            land(layer, 0)

    spot = lax.broadcasted_iota(jnp.int32, (EDGE + 2, EDGE, channels), 1)

    def build_plane(layer, b, dz, z):
        def strip(dx):
            pieces = []
            for dy in (-1, 0, 1):
                t = table[b, 9 * (dz + 1) + 3 * (dy + 1) + (dx + 1)]
                place = jnp.where(t < 0, blank, t * EDGE) + z
                if dz != 0:
                    place = jnp.where(t < bricks, place, edges - bricks + t)
                got = pool[layer, place]
                pieces.append(got[EDGE - 1 :] if dy < 0 else got if dy == 0 else got[:1])
            return jnp.concatenate(pieces, axis=0)

        left, middle, right = strip(-1), strip(0), strip(1)
        before = pltpu.roll(jnp.where(spot == EDGE - 1, left, middle), 1, 1)
        after = pltpu.roll(jnp.where(spot == 0, right, middle), EDGE - 1, 1)
        zp = z + 1 + EDGE * dz
        for j, value in enumerate((before, middle, after)):
            even[j, b, zp] = value.reshape((EDGE + 2) * EDGE, channels).astype(jnp.bfloat16)
            odd[j, b, zp] = value[1:-1].reshape(PLANE, channels).astype(jnp.bfloat16)

    def build_inner(layer, first, count):
        def step(b, carry):
            for z in range(first, first + count):
                build_plane(layer, b, 0, z)
            return carry

        lax.fori_loop(0, bricks, step, 0)

    def build_outer(layer, b):
        build_plane(layer, b, -1, EDGE - 1)
        build_plane(layer, b, 1, 0)

    def operand(b, first, count):
        pieces = []
        for dy in range(3):
            for dx in range(3):
                if dy == 1:
                    piece = odd[dx, b, pl.ds(first, count)]
                else:
                    piece = even[dx, b, pl.ds(first, count), pl.ds(dy * EDGE, PLANE)]
                pieces.append(piece.reshape(count * PLANE, channels))
        return jnp.concatenate(pieces, axis=1)

    def taps_of(layer, dz):
        return w_all[layer, pl.ds(9 * dz, 9)].reshape(9 * channels, channels)

    def middle(layer, b):
        return jnp.dot(
            operand(b, 1, EDGE), taps_of(layer, 1), preferred_element_type=jnp.float32
        )

    def outer(layer, b):
        both = jnp.concatenate([taps_of(layer, 0), taps_of(layer, 2)], axis=1)
        wide = jnp.dot(operand(b, 0, EDGE + 2), both, preferred_element_type=jnp.float32)
        return wide[:voxels, :channels] + wide[2 * PLANE :, channels:]

    def activate(total, b):
        on = jnp.where(table[b, 13] >= 0, 1.0, 0.0)
        return total * (0.5 * on) * (1.0 + jnp.tanh(0.5 * total))

    def gather_weights(layer, parts):
        for part in parts:
            w_own(layer, part, 0).wait_recv()
            w_forward(layer, part).start()
        for part in parts:
            w_own(layer, part, 1).wait_recv()
            w_forward(layer, part).wait()
            w_own(layer, part, 0).wait_send()
            w_own(layer, part, 1).wait_send()

    for i in (0, 4, 5):
        here[i].wait()
    deep = LANES // PLANE
    for i, q in enumerate(ORDER):
        for j in range(3):
            feat_copy(q, j).wait_recv()
        if i == 2:
            send_weights(0, (1,))
        if i == 3:
            send_weights(0, (0, 2))

        def fill(b, carry):
            turned = xt[b, :, pl.ds(q * LANES, LANES)].astype(jnp.float32).T
            pool[0, pl.ds(b * EDGE + q * deep, deep)] = turned.reshape(deep, EDGE, EDGE, channels)
            return carry

        lax.fori_loop(0, bricks, fill, 0)
        if i == 1:
            send_faces(0)
        build_inner(0, q * deep, deep)
    send_weights(1, (1, 0, 2))
    receive_faces(0)
    here[6].wait()
    gather_weights(0, (1,))

    def begin(b, carry):
        acc[b] = middle(0, b)
        build_outer(0, b)
        return carry

    lax.fori_loop(0, bricks, begin, 0)
    gather_weights(0, (0, 2))
    for j in range(3):
        small_copy(j).wait()
    shared = jnp.sum(small_all[...], axis=0)
    row = lax.broadcasted_iota(jnp.int32, shared.shape, 0)
    shift = jnp.sum(jnp.where(row == g, shared, 0.0), axis=0, keepdims=True)
    last = shared[levels : levels + 1]

    def first(b, carry):
        act = activate(acc[b] + outer(0, b) + shift, b).astype(jnp.bfloat16).astype(jnp.float32)
        pool[1, pl.ds(b * EDGE, EDGE)] = act.reshape(EDGE, EDGE, EDGE, channels)
        return carry

    lax.fori_loop(0, bricks, first, 0)
    send_faces(1)
    build_inner(1, 0, EDGE)
    here[7].wait()
    gather_weights(1, (1, 0, 2))
    receive_faces(1)

    def out_copy(b, j):
        return remote(
            staged.at[b, rows(peers[j])], out.at[g, b], out_send.at[b, j], out_recv.at[b, j],
            (s, peers[j]),
        )

    def out_here(b):
        return pltpu.make_async_copy(staged.at[b, rows(g)], out.at[g, b], own_sem.at[b])

    def second(b, carry):
        centre = middle(1, b)
        build_outer(1, b)
        act = activate(centre + outer(1, b) + last, b)
        staged[b] = act.T.astype(jnp.bfloat16)
        for j in range(3):
            out_copy(b, j).start()
        out_here(b).start()
        return carry

    lax.fori_loop(0, bricks, second, 0)

    def finish(b, carry):
        out_here(b).wait()
        for j in range(3):
            out_copy(b, j).wait()
        return carry

    lax.fori_loop(0, bricks, finish, 0)
    for q in ORDER:
        for j in range(3):
            feat_copy(q, j).wait_send()


def shards(features, neighbours, face_lists, weight_first, bias_first, weight_second, bias_second, level_embed):
    levels, bricks, group, voxels = features.shape
    n_chan = lax.axis_size("chan")
    channels = group * n_chan
    face = face_lists.shape[2]
    planes = bricks * EDGE + EDGE + 2 * face
    dma = pltpu.SemaphoreType.DMA
    return pl.pallas_call(
        functools.partial(kernel, lax.axis_size("slab")),
        out_shape=pltpu.VMEM(features.shape, features.dtype),
        in_specs=[pl.BlockSpec(memory_space=pl.ANY)] * 8,
        out_specs=pl.BlockSpec(memory_space=pl.ANY),
        scratch_shapes=[
            pltpu.SMEM(neighbours.shape, jnp.int32),
            pltpu.SMEM(face_lists.shape, jnp.int32),
            pltpu.VMEM((1, group), jnp.float32),
            pltpu.VMEM((1, group), jnp.float32),
            pltpu.VMEM((levels, group), jnp.float32),
            pltpu.VMEM((8, channels), jnp.float32),
            pltpu.VMEM((bricks, channels, voxels), jnp.bfloat16),
            pltpu.VMEM((2, 27, channels, channels), jnp.bfloat16),
            pltpu.VMEM((n_chan, 8, channels), jnp.float32),
            pltpu.VMEM((2, planes, EDGE, EDGE, channels), jnp.float32),
            pltpu.VMEM((3, bricks, EDGE + 2, (EDGE + 2) * EDGE, channels), jnp.bfloat16),
            pltpu.VMEM((3, bricks, EDGE + 2, PLANE, channels), jnp.bfloat16),
            pltpu.VMEM((bricks, voxels, channels), jnp.float32),
            pltpu.VMEM((2, 2, face, PLANE, channels), jnp.bfloat16),
            pltpu.VMEM((2, 2, face, PLANE, channels), jnp.bfloat16),
            pltpu.VMEM((bricks, channels, voxels), jnp.bfloat16),
            dma((4, 3)), dma((4, 3)),
            dma((2, PARTS, 3)), dma((2, PARTS, 3)),
            dma((3,)), dma((3,)),
            dma((2, 2)), dma((2, 2)),
            dma((bricks, 3)), dma((bricks, 3)),
            dma((8,)), dma((bricks,)),
        ],
        compiler_params=pltpu.CompilerParams(
            collective_id=0, has_side_effects=True, vmem_limit_bytes=VMEM_LIMIT
        ),
        cost_estimate=pl.CostEstimate(
            flops=4 * 27 * channels * channels * bricks * voxels,
            bytes_accessed=4 * features.size,
            transcendentals=2 * channels * bricks * voxels,
        ),
    )(
        features, neighbours, face_lists, bias_first[None], bias_second[None], level_embed,
        weight_first.transpose(0, 2, 1), weight_second.transpose(0, 2, 1),
    )


def solution(mesh):
    placed = (
        P(None, "slab", "chan", None),
        P("slab", None),
        P("slab", None, None),
        P(None, None, "chan"),
        P("chan"),
        P(None, None, "chan"),
        P("chan"),
        P(None, "chan"),
    )
    return jax.shard_map(
        shards, mesh=mesh, in_specs=placed, out_specs=P(None, "slab", "chan", None), check_vma=False
    )
```
